32 devices in a mesh: dp: 4 (over z), mp: 8 (over y, x, core).
Axes of the slice: x: 2, y: 2, z: 4, core: 2. Of those that a mesh axis runs over, the one named last changes fastest.
Arguments:
- grad_parts: bfloat16 [4, 8, 512, 10240], P('dp', None, 'mp'), may hold values from -1.1953125 to 1.1953125
- statistics: float32 [2, 5, 4, 8, 512, 512], P(None, None, 'dp', 'mp'), as said below
- prior_roots: bfloat16 [2, 5, 4, 8, 512, 512], P(None, None, 'dp', 'mp'), as said below
- block_order: int32 [160], replicated, may hold values from 0 to 159, each once
Outputs:
- new_statistics: float32 [2, 5, 4, 8, 512, 512], P(None, None, 'dp', 'mp')
- new_roots: bfloat16 [2, 5, 4, 8, 512, 512], P(None, None, 'dp', 'mp')
- update: bfloat16 [8, 512, 10240], P(None, 'mp')
The draws below stay inside these ranges and needn't reach their ends.
Inputs may be any that keep to these rules, and one draw needn't show every extreme that they name: block_order holds every block index once; the block at position j goes to slot position j of the statistics' leading dimensions. `statistics`: each matrix is symmetric positive definite. `prior_roots`: each matrix is symmetric.
All inputs are finite; a program needn't handle non-finite values.
Results may differ from the reference program's by a relative error of at most 0.014.
Values may be sent and summed in bfloat16 or wider, within the bound.
A program may use at most 192 MiB of HBM per device.

```python
import math
import jax
import jax.numpy as jnp
from jax import lax

IN_ROWS = 4096
BLK = 512
ITERS = 2
COLS = 10240
NBLK = 160
SLOTS = 5
N_DP = 4
N_MP = 8


def draw_statistics(key, part):
    key = jax.random.fold_in(key, 11)
    matrix_count = 2 * SLOTS * N_DP * N_MP

    def single_matrix(matrix_index):
        matrix_key = jax.random.fold_in(key, matrix_index)
        first_key, second_key = jax.random.split(matrix_key)
        factor = jax.random.normal(first_key, (BLK, 2 * BLK), jnp.float32)
        row_scale = jnp.exp(jax.random.uniform(second_key, (BLK,), jnp.float32, 0.0, math.log(10.0)))
        product = jnp.dot(factor, factor.T, precision=lax.Precision.HIGHEST) / (2.0 * BLK)
        centre = product + 0.5 * jnp.eye(BLK, dtype=jnp.float32)
        return 0.1 * centre * row_scale[:, None] * row_scale[None, :]
    matrices = lax.map(single_matrix, jnp.arange(matrix_count))
    return matrices.reshape(2, SLOTS, N_DP, N_MP, BLK, BLK)


def draw_prior_roots(key, part):
    key = jax.random.fold_in(key, 23)
    matrix_count = 2 * SLOTS * N_DP * N_MP

    def single_matrix(matrix_index):
        matrix_key = jax.random.fold_in(key, matrix_index)
        first_key, second_key = jax.random.split(matrix_key)
        spread = jax.random.normal(first_key, (BLK, BLK), jnp.float32)
        diagonal = jnp.exp(jax.random.uniform(second_key, (BLK,), jnp.float32, math.log(0.3), 0.0))
        symmetric = (spread + spread.T) * (0.5 / math.sqrt(2.0 * BLK))
        return (symmetric + jnp.diag(diagonal)).astype(jnp.bfloat16)
    matrices = lax.map(single_matrix, jnp.arange(matrix_count))
    return matrices.reshape(2, SLOTS, N_DP, N_MP, BLK, BLK)


def steps_of(key, shape, cuts, low, top_value):
    gain, own = 1.0, jax.random.fold_in(key, 6)
    for position, blocks in cuts:
        heights = jnp.exp(jax.random.uniform(jax.random.fold_in(own, position), (blocks,), jnp.float32, low / len(cuts), top_value / len(cuts)))
        gain = gain * jnp.repeat(heights, shape[position] // blocks).reshape([-1 if axis == position else 1 for axis in range(len(shape))])
    return gain


def bell_draw(own_key, dims, deviation, reach, cuts=(), kind=jnp.bfloat16):
    array = deviation * jax.random.normal(own_key, dims, jnp.float32)
    if cuts:
        array = array * steps_of(own_key, dims, cuts, -0.22, 0.18)
    return jnp.clip(array, -reach, reach).astype(kind)


def setup_inputs(seed: int = 0) -> dict:
    arg_keys = jax.random.split(jax.random.key(seed), 5)
    grad_parts = bell_draw(arg_keys[0], (N_DP, IN_ROWS // BLK, BLK, COLS), 0.2, 1.1953125, ((0, 4), (2, 8)))
    statistics = draw_statistics(jax.random.fold_in(arg_keys[4], 71), 0)
    prior_roots = draw_prior_roots(jax.random.fold_in(arg_keys[4], 71), 0)
    block_order = jax.random.permutation(arg_keys[3], NBLK).astype(jnp.int32)
    return dict(grad_parts=grad_parts, statistics=statistics, prior_roots=prior_roots, block_order=block_order)


DECAY = 0.95

def inverse_root(matrix):
    identity = jnp.eye(matrix.shape[0], dtype=jnp.float32)
    magnitude = jnp.sqrt(jnp.sum(matrix * matrix)) + 1e-06
    current = matrix / magnitude
    iterate = identity * magnitude ** (-0.25)
    for iteration in range(ITERS):
        factor = (5.0 * identity - current) / 4.0
        iterate = jnp.dot(iterate, factor, precision=lax.Precision.HIGHEST)
        if iteration + 1 < ITERS:
            square = jnp.dot(factor, factor, precision=lax.Precision.HIGHEST)
            fourth = jnp.dot(square, square, precision=lax.Precision.HIGHEST)
            current = jnp.dot(fourth, current, precision=lax.Precision.HIGHEST)
    return iterate

def owner_work(operands):
    left_stat, right_stat, left_root, right_root, block_grad = operands
    left_gram = jnp.dot(block_grad, block_grad.T, preferred_element_type=jnp.float32)
    right_gram = jnp.dot(block_grad.T, block_grad, preferred_element_type=jnp.float32)
    new_left = DECAY * left_stat + (1.0 - DECAY) * left_gram
    new_right = DECAY * right_stat + (1.0 - DECAY) * right_gram
    scaled = jnp.dot(left_root, block_grad, preferred_element_type=jnp.float32).astype(jnp.bfloat16)
    update = jnp.dot(scaled, right_root, preferred_element_type=jnp.float32).astype(jnp.bfloat16)
    root_left = inverse_root(new_left).astype(jnp.bfloat16)
    root_right = inverse_root(new_right).astype(jnp.bfloat16)
    return (new_left, new_right, root_left, root_right, update)

def reference(grad_parts, statistics, prior_roots, block_order):
    summed_grad = lax.optimization_barrier(jnp.sum(grad_parts.astype(jnp.float32), axis=0)).astype(jnp.bfloat16)
    block_rows = IN_ROWS // BLK
    block_cols = COLS // BLK
    grad_tiles = summed_grad.reshape(block_rows, BLK, block_cols, BLK).transpose(0, 2, 1, 3).reshape(NBLK, BLK, BLK)
    positions = SLOTS * N_DP * N_MP
    flat_stats = statistics.reshape(2, positions, BLK, BLK)
    flat_roots = prior_roots.reshape(2, positions, BLK, BLK)
    owned = grad_tiles[block_order]
    new_left, new_right, root_left, root_right, updates = lax.map(owner_work, (flat_stats[0, :NBLK], flat_stats[1, :NBLK], flat_roots[0, :NBLK], flat_roots[1, :NBLK], owned))
    empty_count = positions - NBLK
    stat_zeros = jnp.zeros((empty_count, BLK, BLK), jnp.float32)
    root_zeros = jnp.zeros((empty_count, BLK, BLK), jnp.bfloat16)
    new_statistics = jnp.stack([jnp.concatenate([new_left, stat_zeros], axis=0), jnp.concatenate([new_right, stat_zeros], axis=0)]).reshape(statistics.shape)
    new_roots = jnp.stack([jnp.concatenate([root_left, root_zeros], axis=0), jnp.concatenate([root_right, root_zeros], axis=0)]).reshape(prior_roots.shape)
    inverse_order = jnp.argsort(block_order)
    block_updates = updates[inverse_order]
    update = block_updates.reshape(block_rows, block_cols, BLK, BLK).transpose(0, 2, 1, 3).reshape(block_rows, BLK, COLS)
    return (new_statistics, new_roots, update)
```

```python
import functools

import jax
import jax.numpy as jnp
from jax import lax
from jax.experimental import pallas as pl
from jax.experimental.pallas import tpu as pltpu
from jax.sharding import PartitionSpec as P

DECAY = 0.95
MESH = pl.DeviceIdType.MESH
COEFS = (
    25.0 / 16.0,
    -5.0 / 16.0 - 3125.0 / 4096.0,
    3125.0 / 4096.0,
    -1250.0 / 4096.0,
    250.0 / 4096.0,
    -25.0 / 4096.0,
    1.0 / 4096.0,
)


def gather_kernel(order_ref, grad_ref, out_ref, sem):
    count, _, width = out_ref.shape
    per_row = grad_ref.shape[3] // width

    def issue(j, carry):
        block = order_ref[j]
        column = pl.multiple_of((block % per_row) * width, width)
        pltpu.make_async_copy(
            grad_ref.at[0, block // per_row, :, pl.ds(column, width)], out_ref.at[j], sem
        ).start()
        return carry

    lax.fori_loop(0, count, issue, 0)
    pltpu.make_async_copy(out_ref, out_ref, sem).wait()


def scatter_kernel(order_ref, tiles_ref, out_ref, sem):
    count = order_ref.shape[0]
    width = tiles_ref.shape[2]
    per_row = out_ref.shape[2] // width

    def issue(j, carry):
        block = order_ref[j]
        column = pl.multiple_of((block % per_row) * width, width)
        pltpu.make_async_copy(
            tiles_ref.at[j], out_ref.at[block // per_row, :, pl.ds(column, width)], sem
        ).start()
        return carry

    lax.fori_loop(0, count, issue, 0)
    pltpu.make_async_copy(out_ref, out_ref, sem).wait()


def dot(a, b, dims=((1,), (0,))):
    return lax.dot_general(a, b, (dims, ((), ())), preferred_element_type=jnp.float32)


def inverse_root(matrix):
    magnitude = jnp.sqrt(jnp.sum(matrix * matrix, keepdims=True)) + 1e-06
    m1 = matrix * (1.0 / magnitude)
    scale = lax.rsqrt(jnp.sqrt(magnitude))
    h1 = m1.astype(jnp.bfloat16)
    m2 = dot(h1, h1)
    m3 = dot(h1, m2.astype(jnp.bfloat16))
    high = COEFS[4] * m1 + COEFS[5] * m2 + COEFS[6] * m3
    top = dot(m3.astype(jnp.bfloat16), high.astype(jnp.bfloat16))
    size = matrix.shape[0]
    diagonal = lax.broadcasted_iota(jnp.int32, (size, size), 0) == lax.broadcasted_iota(
        jnp.int32, (size, size), 1
    )
    total = top + COEFS[1] * m1 + COEFS[2] * m2 + COEFS[3] * m3
    total = total + jnp.where(diagonal, COEFS[0], 0.0)
    return total * scale


def step_kernel(
    slots, dn, mn, block_count,
    pieces, stats_in, roots_in,
    stats_out, roots_out, gathered,
    recv, summed, grads, upd, stats, roots,
    rs_send, rs_recv, a1_send, a1_recv, a2_send, a2_recv, ag_send, ag_recv,
    in_sem, out_sem,
):
    d = lax.axis_index("dp")
    m = lax.axis_index("mp")
    rows = grads.shape[1] // mn

    barrier = pltpu.get_barrier_semaphore()

    def greet(k, carry):
        pl.semaphore_signal(barrier, inc=1, device_id=(d, lax.rem(m + k, mn)), device_id_type=MESH)
        return carry

    lax.fori_loop(1, mn, greet, 0)

    @pl.when(d > 0)
    def _():
        pl.semaphore_signal(barrier, inc=1, device_id=(d - 1, m), device_id_type=MESH)

    @pl.when(d < dn - 1)
    def _():
        pl.semaphore_signal(barrier, inc=1, device_id=(d + 1, m), device_id_type=MESH)

    def stat_in(s, side):
        return pltpu.make_async_copy(stats_in.at[side, s], stats.at[side, s], in_sem.at[s, side])

    def root_in(s, side):
        return pltpu.make_async_copy(roots_in.at[side, s], roots.at[side, s], in_sem.at[s, 2 + side])

    def stat_out(s, side):
        return pltpu.make_async_copy(stats.at[side, s], stats_out.at[side, s], out_sem.at[s, side])

    def root_out(s, side):
        return pltpu.make_async_copy(roots.at[side, s], roots_out.at[side, s], out_sem.at[s, 2 + side])

    def fetch(s, carry):
        for side in range(2):
            root_in(s, side).start()
            stat_in(s, side).start()
        return carry

    lax.fori_loop(0, slots, fetch, 0)

    ends = (d == 0).astype(jnp.int32) + (d == dn - 1).astype(jnp.int32)
    pl.semaphore_wait(barrier, mn + 1 - ends)

    def rs_copy(s, o, step, first):
        place = o + 1 if step > 0 else o
        return pltpu.make_async_remote_copy(
            src_ref=pieces.at[s, o] if first else recv.at[s, place],
            dst_ref=recv.at[s, place],
            send_sem=rs_send.at[s, place],
            recv_sem=rs_recv.at[s, place],
            device_id=(d + step, m),
            device_id_type=MESH,
        )

    def ag_copy(s, o, step):
        return pltpu.make_async_remote_copy(
            src_ref=gathered.at[s, o],
            dst_ref=gathered.at[s, o],
            send_sem=ag_send.at[s, o, 1 if step > 0 else 0],
            recv_sem=ag_recv.at[s, o],
            device_id=(d + step, m),
            device_id_type=MESH,
        )

    def rows_of(k):
        return pl.ds(pl.multiple_of(k * rows, rows), rows)

    def a1_copy(s, k):
        return pltpu.make_async_remote_copy(
            src_ref=summed.at[s, rows_of(k)],
            dst_ref=grads.at[s, rows_of(m)],
            send_sem=a1_send.at[s, k],
            recv_sem=a1_recv.at[s, m],
            device_id=(d, k),
            device_id_type=MESH,
        )

    def a2_copy(s, k):
        return pltpu.make_async_remote_copy(
            src_ref=upd.at[s, rows_of(k)],
            dst_ref=gathered.at[s, d, rows_of(m)],
            send_sem=a2_send.at[s, k],
            recv_sem=a2_recv.at[s, m],
            device_id=(d, k),
            device_id_type=MESH,
        )

    def a1_arrival(s, k):
        return pltpu.make_async_copy(grads.at[s, rows_of(k)], grads.at[s, rows_of(k)], a1_recv.at[s, k])

    def a2_arrival(s, k):
        return pltpu.make_async_copy(
            gathered.at[s, d, rows_of(k)], gathered.at[s, d, rows_of(k)], a2_recv.at[s, k]
        )

    def peers(action):
        def body(k, carry):
            action(lax.rem(m + k, mn))
            return carry

        lax.fori_loop(1, mn, body, 0)

    def add_pieces(s, o, place):
        recv[s, place] = (
            recv[s, place].astype(jnp.float32) + pieces[s, o].astype(jnp.float32)
        ).astype(jnp.bfloat16)

    def rs_start(s):
        @pl.when(d == 0)
        def _():
            for o in range(dn - 1, 0, -1):
                rs_copy(s, o, 1, True).start()

        @pl.when(d == dn - 1)
        def _():
            for o in range(dn - 1):
                rs_copy(s, o, -1, True).start()

    def relay(s, rank):
        right, left = dn - 1 - rank, rank

        @pl.when((s < slots) & (d > 0) & (d < right))
        def _():
            rs_copy(s, right, 1, False).wait_recv()
            add_pieces(s, right, right + 1)
            rs_copy(s, right, 1, False).start()

        @pl.when((s < slots) & (d < dn - 1) & (d > left))
        def _():
            rs_copy(s, left, -1, False).wait_recv()
            add_pieces(s, left, left)
            rs_copy(s, left, -1, False).start()

        near_left, near_right = d - 1 - rank, d + 1 + rank

        @pl.when((s > 0) & (d < dn - 1) & (near_left >= 0))
        def _():
            ag_copy(s - 1, near_left, 1).wait_recv()
            ag_copy(s - 1, near_left, 1).start()

        @pl.when((s > 0) & (d > 0) & (near_right < dn))
        def _():
            ag_copy(s - 1, near_right, -1).wait_recv()
            ag_copy(s - 1, near_right, -1).start()

    def own(s):
        @pl.when(d > 0)
        def _():
            rs_copy(s, d, 1, False).wait_recv()

        @pl.when(d < dn - 1)
        def _():
            rs_copy(s, d, -1, False).wait_recv()

        @pl.when(d == 0)
        def _():
            summed[s] = (
                recv[s, d].astype(jnp.float32) + pieces[s, d].astype(jnp.float32)
            ).astype(jnp.bfloat16)

        @pl.when(d == dn - 1)
        def _():
            summed[s] = (
                recv[s, d + 1].astype(jnp.float32) + pieces[s, d].astype(jnp.float32)
            ).astype(jnp.bfloat16)

        @pl.when((d > 0) & (d < dn - 1))
        def _():
            summed[s] = (
                recv[s, d].astype(jnp.float32)
                + recv[s, d + 1].astype(jnp.float32)
                + pieces[s, d].astype(jnp.float32)
            ).astype(jnp.bfloat16)

        peers(lambda k: a1_copy(s, k).start())
        grads[s, rows_of(m)] = summed[s, rows_of(m)]
        for side in range(2):
            root_in(s, side).wait()
        peers(lambda k: a1_arrival(s, k).wait())
        scaled = dot(roots[0, s], grads[s]).astype(jnp.bfloat16)
        upd[s] = dot(scaled, roots[1, s]).astype(jnp.bfloat16)
        peers(lambda k: a2_copy(s, k).start())
        mine = pltpu.make_async_copy(
            upd.at[s, rows_of(m)], gathered.at[s, d, rows_of(m)], a2_send.at[s, m]
        )
        mine.start()
        mine.wait()
        peers(lambda k: a2_arrival(s, k).wait())

        @pl.when(d < dn - 1)
        def _():
            ag_copy(s, d, 1).start()

        @pl.when(d > 0)
        def _():
            ag_copy(s, d, -1).start()

    def statistic(s, side):
        live = (s * dn + d) * mn + m < block_count
        stat_in(s, side).wait()
        block = grads[s]
        gram = dot(block, block, ((1 - side,), (1 - side,)))
        new = DECAY * stats[side, s] + (1.0 - DECAY) * gram
        stats[side, s] = jnp.where(live, new, 0.0)
        root = inverse_root(new)
        roots[side, s] = jnp.where(live, root, 0.0).astype(jnp.bfloat16)
        stat_out(s, side).start()
        root_out(s, side).start()

    rs_start(0)

    def step(s, carry):
        @pl.when(s + 1 < slots)
        def _():
            rs_start(s + 1)

        for rank in range(dn - 1):
            relay(s, rank)

        @pl.when(s < slots)
        def _():
            own(s)
            for side in range(2):
                statistic(s, side)

        return carry

    lax.fori_loop(0, slots + 1, step, 0)

    def finish(s, carry):
        for side in range(2):
            stat_out(s, side).wait()
            root_out(s, side).wait()
        peers(lambda k: a1_copy(s, k).wait_send())
        peers(lambda k: a2_copy(s, k).wait_send())
        for o in range(dn):
            @pl.when(o > d)
            def _():
                rs_copy(s, o, 1, False).wait_send()

            @pl.when(o < d)
            def _():
                rs_copy(s, o, -1, False).wait_send()

            @pl.when((o <= d) & (d < dn - 1))
            def _():
                ag_copy(s, o, 1).wait_send()

            @pl.when((o >= d) & (d > 0))
            def _():
                ag_copy(s, o, -1).wait_send()

            @pl.when((o < d) & (d == dn - 1))
            def _():
                ag_copy(s, o, 1).wait_recv()

            @pl.when((o > d) & (d == 0))
            def _():
                ag_copy(s, o, -1).wait_recv()

        return carry

    lax.fori_loop(0, slots, finish, 0)


def shards(grad_parts, statistics, prior_roots, block_order):
    dn = lax.axis_size("dp")
    mn = lax.axis_size("mp")
    width = statistics.shape[-1]
    slots = statistics.shape[1]
    rows = grad_parts.shape[2]
    block_count = block_order.shape[0]
    positions = slots * dn * mn
    chosen = block_order
    if positions > block_count:
        chosen = jnp.pad(block_order, (0, positions - block_count))
    anywhere = pl.BlockSpec(memory_space=pl.ANY)
    indices = pl.BlockSpec(memory_space=pltpu.SMEM)
    tile_bytes = positions * rows * width * 2
    pieces = pl.pallas_call(
        gather_kernel,
        out_shape=jax.ShapeDtypeStruct((positions, rows, width), jnp.bfloat16),
        in_specs=[indices, anywhere],
        out_specs=anywhere,
        scratch_shapes=[pltpu.SemaphoreType.DMA],
        cost_estimate=pl.CostEstimate(flops=0, bytes_accessed=2 * tile_bytes, transcendentals=0),
    )(chosen, grad_parts)
    pieces = pieces.reshape(slots, dn, width, width)
    dma = pltpu.SemaphoreType.DMA
    block = (width, width)
    new_stats, new_roots, gathered = pl.pallas_call(
        functools.partial(step_kernel, slots, dn, mn, block_count),
        out_shape=(
            jax.ShapeDtypeStruct((2, slots) + block, jnp.float32),
            jax.ShapeDtypeStruct((2, slots) + block, jnp.bfloat16),
            jax.ShapeDtypeStruct((slots, dn) + block, jnp.bfloat16),
        ),
        in_specs=[pl.BlockSpec(memory_space=pltpu.VMEM), anywhere, anywhere],
        out_specs=(anywhere, anywhere, anywhere),
        scratch_shapes=[
            pltpu.VMEM((slots, dn + 1) + block, jnp.bfloat16),
            pltpu.VMEM((slots,) + block, jnp.bfloat16),
            pltpu.VMEM((slots,) + block, jnp.bfloat16),
            pltpu.VMEM((slots,) + block, jnp.bfloat16),
            pltpu.VMEM((2, slots) + block, jnp.float32),
            pltpu.VMEM((2, slots) + block, jnp.bfloat16),
            dma((slots, dn + 1)),
            dma((slots, dn + 1)),
            dma((slots, mn)),
            dma((slots, mn)),
            dma((slots, mn)),
            dma((slots, mn)),
            dma((slots, dn, 2)),
            dma((slots, dn)),
            dma((slots, 4)),
            dma((slots, 4)),
        ],
        compiler_params=pltpu.CompilerParams(
            collective_id=0, has_side_effects=True, vmem_limit_bytes=60 * 1024 * 1024
        ),
        cost_estimate=pl.CostEstimate(
            flops=slots * 20 * width**3, bytes_accessed=10 * tile_bytes, transcendentals=0
        ),
    )(
        pieces,
        statistics.reshape((2, slots) + block),
        prior_roots.reshape((2, slots) + block),
    )
    update = pl.pallas_call(
        scatter_kernel,
        out_shape=jax.ShapeDtypeStruct(grad_parts.shape[1:], jnp.bfloat16),
        in_specs=[indices, anywhere],
        out_specs=anywhere,
        scratch_shapes=[pltpu.SemaphoreType.DMA],
        cost_estimate=pl.CostEstimate(flops=0, bytes_accessed=2 * tile_bytes, transcendentals=0),
    )(block_order, gathered.reshape(positions, rows, width))
    return (
        new_stats.reshape(statistics.shape),
        new_roots.reshape(prior_roots.shape),
        update,
    )


def solution(mesh):
    placed = (
        P("dp", None, "mp", None),
        P(None, None, "dp", "mp", None, None),
        P(None, None, "dp", "mp", None, None),
        P(),
    )
    return jax.shard_map(
        shards,
        mesh=mesh,
        in_specs=placed,
        out_specs=(
            P(None, None, "dp", "mp", None, None),
            P(None, None, "dp", "mp", None, None),
            P(None, "mp", None),
        ),
        check_vma=False,
    )
```

```python
import functools

import jax
import jax.numpy as jnp
from jax import lax
from jax.experimental import pallas as pl
from jax.experimental.pallas import tpu as pltpu
from jax.sharding import PartitionSpec as P

DECAY = 0.95
MESH = pl.DeviceIdType.MESH
COEFS = (
    25.0 / 16.0,
    -5.0 / 16.0 - 3125.0 / 4096.0,
    3125.0 / 4096.0,
    -1250.0 / 4096.0,
    250.0 / 4096.0,
    -25.0 / 4096.0,
    1.0 / 4096.0,
)


def scatter_kernel(order_ref, tiles_ref, out_ref, sem):
    count = order_ref.shape[0]
    width = tiles_ref.shape[2]
    per_row = out_ref.shape[2] // width

    def issue(j, carry):
        block = order_ref[j]
        column = pl.multiple_of((block % per_row) * width, width)
        pltpu.make_async_copy(
            tiles_ref.at[j], out_ref.at[block // per_row, :, pl.ds(column, width)], sem
        ).start()
        return carry

    lax.fori_loop(0, count, issue, 0)
    pltpu.make_async_copy(out_ref, out_ref, sem).wait()


def dot(a, b, dims=((1,), (0,))):
    return lax.dot_general(a, b, (dims, ((), ())), preferred_element_type=jnp.float32)


def inverse_root(matrix):
    magnitude = jnp.sqrt(jnp.sum(matrix * matrix, keepdims=True)) + 1e-06
    m1 = matrix * (1.0 / magnitude)
    scale = lax.rsqrt(jnp.sqrt(magnitude))
    h1 = m1.astype(jnp.bfloat16)
    m2 = dot(h1, h1)
    m3 = dot(h1, m2.astype(jnp.bfloat16))
    high = COEFS[4] * m1 + COEFS[5] * m2 + COEFS[6] * m3
    top = dot(m3.astype(jnp.bfloat16), high.astype(jnp.bfloat16))
    size = matrix.shape[0]
    diagonal = lax.broadcasted_iota(jnp.int32, (size, size), 0) == lax.broadcasted_iota(
        jnp.int32, (size, size), 1
    )
    total = top + COEFS[1] * m1 + COEFS[2] * m2 + COEFS[3] * m3
    total = total + jnp.where(diagonal, COEFS[0], 0.0)
    return total * scale


def step_kernel(
    slots, dn, mn, block_count,
    order, grad_in, stats_in, roots_in,
    stats_out, roots_out, gathered_out,
    parts, recv, gathered, grads, stats, roots,
    rs_send, rs_recv, a1_send, a1_recv, a2_send, a2_recv, ag_send, ag_recv,
    in_sem, out_sem, part_sem, tile_sem,
):
    d = lax.axis_index("dp")
    m = lax.axis_index("mp")
    rows = grads.shape[1] // mn
    width = grads.shape[2]
    per_row = grad_in.shape[3] // width

    def pick(block, carry):
        column = pl.multiple_of((block % per_row) * width, width)
        pltpu.make_async_copy(
            grad_in.at[0, block // per_row, :, pl.ds(column, width)], parts.at[block], part_sem
        ).start()
        return carry

    lax.fori_loop(0, parts.shape[0], pick, 0)

    barrier = pltpu.get_barrier_semaphore()

    def greet(k, carry):
        pl.semaphore_signal(barrier, inc=1, device_id=(d, lax.rem(m + k, mn)), device_id_type=MESH)
        return carry

    lax.fori_loop(1, mn, greet, 0)

    @pl.when(d > 0)
    def _():
        pl.semaphore_signal(barrier, inc=1, device_id=(d - 1, m), device_id_type=MESH)

    @pl.when(d < dn - 1)
    def _():
        pl.semaphore_signal(barrier, inc=1, device_id=(d + 1, m), device_id_type=MESH)

    def stat_in(s, side):
        return pltpu.make_async_copy(stats_in.at[side, s], stats.at[side, s], in_sem.at[s, side])

    def root_in(s, side):
        return pltpu.make_async_copy(roots_in.at[side, s], roots.at[side, s], in_sem.at[s, 2 + side])

    def stat_out(s, side):
        return pltpu.make_async_copy(stats.at[side, s], stats_out.at[side, s], out_sem.at[s, side])

    def root_out(s, side):
        return pltpu.make_async_copy(roots.at[side, s], roots_out.at[side, s], out_sem.at[s, 2 + side])

    def fetch(s, carry):
        for side in range(2):
            root_in(s, side).start()
            stat_in(s, side).start()
        return carry

    lax.fori_loop(0, slots, fetch, 0)

    ends = (d == 0).astype(jnp.int32) + (d == dn - 1).astype(jnp.int32)
    pl.semaphore_wait(barrier, mn + 1 - ends)

    pltpu.make_async_copy(parts, parts, part_sem).wait()

    def rs_copy(s, o, step):
        place = o + 1 if step > 0 else o
        return pltpu.make_async_remote_copy(
            src_ref=recv.at[s, place],
            dst_ref=recv.at[s, place],
            send_sem=rs_send.at[s, place],
            recv_sem=rs_recv.at[s, place],
            device_id=(d + step, m),
            device_id_type=MESH,
        )

    def ag_copy(s, o, step):
        return pltpu.make_async_remote_copy(
            src_ref=gathered.at[s, o],
            dst_ref=gathered.at[s, o],
            send_sem=ag_send.at[s, o, 1 if step > 0 else 0],
            recv_sem=ag_recv.at[s, o],
            device_id=(d + step, m),
            device_id_type=MESH,
        )

    def rows_of(k):
        return pl.ds(pl.multiple_of(k * rows, rows), rows)

    def a1_copy(s, k):
        return pltpu.make_async_remote_copy(
            src_ref=recv.at[s, d, rows_of(k)],
            dst_ref=grads.at[s, rows_of(m)],
            send_sem=a1_send.at[s, k],
            recv_sem=a1_recv.at[s, m],
            device_id=(d, k),
            device_id_type=MESH,
        )

    def a2_copy(s, k):
        return pltpu.make_async_remote_copy(
            src_ref=recv.at[s, d + 1, rows_of(k)],
            dst_ref=gathered.at[s, d, rows_of(m)],
            send_sem=a2_send.at[s, k],
            recv_sem=a2_recv.at[s, m],
            device_id=(d, k),
            device_id_type=MESH,
        )

    def a1_arrival(s, k):
        return pltpu.make_async_copy(grads.at[s, rows_of(k)], grads.at[s, rows_of(k)], a1_recv.at[s, k])

    def a2_arrival(s, k):
        return pltpu.make_async_copy(
            gathered.at[s, d, rows_of(k)], gathered.at[s, d, rows_of(k)], a2_recv.at[s, k]
        )

    def peers(action):
        def body(k, carry):
            action(lax.rem(m + k, mn))
            return carry

        lax.fori_loop(1, mn, body, 0)

    def add_pieces(s, o, target, *terms):
        def body(p, carry):
            piece = parts[order[(s * dn + o) * mn + p]]
            at = rows_of(p)
            if terms:
                total = piece.astype(jnp.float32)
                for t in terms:
                    total = total + recv[s, t, at].astype(jnp.float32)
                piece = total.astype(jnp.bfloat16)
            recv[s, target, at] = piece
            return carry

        lax.fori_loop(0, mn, body, 0)

    def rs_start(s, rank):
        right, left = dn - 1 - rank, rank

        @pl.when((s < slots) & (d == 0))
        def _():
            add_pieces(s, right, right + 1)

            @pl.when(s > 0)
            def _():
                rs_copy(s - 1, right, 1).wait_send()

            rs_copy(s, right, 1).start()

        @pl.when((s < slots) & (d == dn - 1))
        def _():
            add_pieces(s, left, left)

            @pl.when(s > 0)
            def _():
                rs_copy(s - 1, left, -1).wait_send()

            rs_copy(s, left, -1).start()

    def relay(s, rank):
        right, left = dn - 1 - rank, rank

        @pl.when((s < slots) & (d > 0) & (d < right))
        def _():
            rs_copy(s, right, 1).wait_recv()
            add_pieces(s, right, right + 1, right + 1)
            rs_copy(s, right, 1).start()

        @pl.when((s < slots) & (d < dn - 1) & (d > left))
        def _():
            rs_copy(s, left, -1).wait_recv()
            add_pieces(s, left, left, left)
            rs_copy(s, left, -1).start()

        near_left, near_right = d - 1 - rank, d + 1 + rank

        @pl.when((s > 0) & (d < dn - 1) & (near_left >= 0))
        def _():
            ag_copy(s - 1, near_left, 1).wait_recv()
            ag_copy(s - 1, near_left, 1).start()

        @pl.when((s > 0) & (d > 0) & (near_right < dn))
        def _():
            ag_copy(s - 1, near_right, -1).wait_recv()
            ag_copy(s - 1, near_right, -1).start()

    def own(s):
        @pl.when(d > 0)
        def _():
            rs_copy(s, d, 1).wait_recv()

        @pl.when(d < dn - 1)
        def _():
            rs_copy(s, d, -1).wait_recv()

        @pl.when(d == 0)
        def _():
            add_pieces(s, d, d, d)

        @pl.when(d == dn - 1)
        def _():
            add_pieces(s, d, d, d + 1)

        @pl.when((d > 0) & (d < dn - 1))
        def _():
            add_pieces(s, d, d, d, d + 1)

        peers(lambda k: a1_copy(s, k).start())
        grads[s, rows_of(m)] = recv[s, d, rows_of(m)]
        for side in range(2):
            root_in(s, side).wait()
        peers(lambda k: a1_arrival(s, k).wait())
        scaled = dot(roots[0, s], grads[s]).astype(jnp.bfloat16)
        recv[s, d + 1] = dot(scaled, roots[1, s]).astype(jnp.bfloat16)
        peers(lambda k: a2_copy(s, k).start())
        gathered[s, d, rows_of(m)] = recv[s, d + 1, rows_of(m)]
        peers(lambda k: a2_arrival(s, k).wait())

        @pl.when(d < dn - 1)
        def _():
            ag_copy(s, d, 1).start()

        @pl.when(d > 0)
        def _():
            ag_copy(s, d, -1).start()

    def statistic(s, side):
        live = (s * dn + d) * mn + m < block_count
        stat_in(s, side).wait()
        block = grads[s]
        gram = dot(block, block, ((1 - side,), (1 - side,)))
        new = DECAY * stats[side, s] + (1.0 - DECAY) * gram
        stats[side, s] = jnp.where(live, new, 0.0)
        root = inverse_root(new)
        roots[side, s] = jnp.where(live, root, 0.0).astype(jnp.bfloat16)
        stat_out(s, side).start()
        root_out(s, side).start()

    for rank in range(dn - 1):
        rs_start(0, rank)

    def step(s, carry):
        for rank in range(dn - 1):
            rs_start(s + 1, rank)
            relay(s, rank)
            if rank < 2:
                @pl.when(s > 0)
                def _():
                    statistic(s - 1, rank)

        @pl.when(s < slots)
        def _():
            own(s)

        return carry

    lax.fori_loop(0, slots + 1, step, 0)

    def tile_out(s):
        return pltpu.make_async_copy(gathered.at[s], gathered_out.at[s], tile_sem.at[s])

    def finish(s, carry):
        for o in range(dn):
            @pl.when((o < d) & (d == dn - 1))
            def _():
                ag_copy(s, o, 1).wait_recv()

            @pl.when((o > d) & (d == 0))
            def _():
                ag_copy(s, o, -1).wait_recv()

        tile_out(s).start()
        for side in range(2):
            stat_out(s, side).wait()
            root_out(s, side).wait()
        peers(lambda k: a1_copy(s, k).wait_send())
        peers(lambda k: a2_copy(s, k).wait_send())
        for o in range(dn):
            @pl.when((o > d) & ((d > 0) | (s == slots - 1)))
            def _():
                rs_copy(s, o, 1).wait_send()

            @pl.when((o < d) & ((d < dn - 1) | (s == slots - 1)))
            def _():
                rs_copy(s, o, -1).wait_send()

            @pl.when((o <= d) & (d < dn - 1))
            def _():
                ag_copy(s, o, 1).wait_send()

            @pl.when((o >= d) & (d > 0))
            def _():
                ag_copy(s, o, -1).wait_send()

        return carry

    lax.fori_loop(0, slots, finish, 0)

    def drain(s, carry):
        tile_out(s).wait()
        return carry

    lax.fori_loop(0, slots, drain, 0)


def shards(grad_parts, statistics, prior_roots, block_order):
    dn = lax.axis_size("dp")
    mn = lax.axis_size("mp")
    width = statistics.shape[-1]
    slots = statistics.shape[1]
    rows = grad_parts.shape[2]
    block_count = block_order.shape[0]
    positions = slots * dn * mn
    chosen = block_order
    if positions > block_count:
        chosen = jnp.pad(block_order, (0, positions - block_count))
    anywhere = pl.BlockSpec(memory_space=pl.ANY)
    indices = pl.BlockSpec(memory_space=pltpu.SMEM)
    tile_bytes = positions * rows * width * 2
    dma = pltpu.SemaphoreType.DMA
    block = (width, width)
    new_stats, new_roots, gathered = pl.pallas_call(
        functools.partial(step_kernel, slots, dn, mn, block_count),
        out_shape=(
            jax.ShapeDtypeStruct((2, slots) + block, jnp.float32),
            jax.ShapeDtypeStruct((2, slots) + block, jnp.bfloat16),
            jax.ShapeDtypeStruct((slots, dn) + block, jnp.bfloat16),
        ),
        in_specs=[indices, anywhere, anywhere, anywhere],
        out_specs=(anywhere, anywhere, anywhere),
        scratch_shapes=[
            pltpu.VMEM((block_count, rows, width), jnp.bfloat16),
            pltpu.VMEM((slots, dn + 1) + block, jnp.bfloat16),
            pltpu.VMEM((slots, dn) + block, jnp.bfloat16),
            pltpu.VMEM((slots,) + block, jnp.bfloat16),
            pltpu.VMEM((2, slots) + block, jnp.float32),
            pltpu.VMEM((2, slots) + block, jnp.bfloat16),
            dma((slots, dn + 1)),
            dma((slots, dn + 1)),
            dma((slots, mn)),
            dma((slots, mn)),
            dma((slots, mn)),
            dma((slots, mn)),
            dma((slots, dn, 2)),
            dma((slots, dn)),
            dma((slots, 4)),
            dma((slots, 4)),
            dma,
            dma((slots,)),
        ],
        compiler_params=pltpu.CompilerParams(
            collective_id=0, has_side_effects=True, vmem_limit_bytes=62 * 1024 * 1024
        ),
        cost_estimate=pl.CostEstimate(
            flops=slots * 20 * width**3, bytes_accessed=10 * tile_bytes, transcendentals=0
        ),
    )(
        chosen,
        grad_parts,
        statistics.reshape((2, slots) + block),
        prior_roots.reshape((2, slots) + block),
    )
    update = pl.pallas_call(
        scatter_kernel,
        out_shape=jax.ShapeDtypeStruct(grad_parts.shape[1:], jnp.bfloat16),
        in_specs=[indices, anywhere],
        out_specs=pl.BlockSpec(memory_space=pltpu.VMEM),
        scratch_shapes=[pltpu.SemaphoreType.DMA],
        compiler_params=pltpu.CompilerParams(vmem_limit_bytes=40 * 1024 * 1024),
        cost_estimate=pl.CostEstimate(flops=0, bytes_accessed=2 * tile_bytes, transcendentals=0),
    )(block_order, gathered.reshape(positions, rows, width))
    return (
        new_stats.reshape(statistics.shape),
        new_roots.reshape(prior_roots.shape),
        update,
    )


def solution(mesh):
    placed = (
        P("dp", None, "mp", None),
        P(None, None, "dp", "mp", None, None),
        P(None, None, "dp", "mp", None, None),
        P(),
    )
    return jax.shard_map(
        shards,
        mesh=mesh,
        in_specs=placed,
        out_specs=(
            P(None, None, "dp", "mp", None, None),
            P(None, None, "dp", "mp", None, None),
            P(None, "mp", None),
        ),
        check_vma=False,
    )
```

```python
import functools

import jax
import jax.numpy as jnp
from jax import lax
from jax.experimental import pallas as pl
from jax.experimental.pallas import tpu as pltpu
from jax.sharding import PartitionSpec as P

DECAY = 0.95
MESH = pl.DeviceIdType.MESH
COEFS = (
    25.0 / 16.0,
    -5.0 / 16.0 - 3125.0 / 4096.0,
    3125.0 / 4096.0,
    -1250.0 / 4096.0,
    250.0 / 4096.0,
    -25.0 / 4096.0,
    1.0 / 4096.0,
)


def scatter_kernel(order_ref, tiles_ref, out_ref, sem):
    count = order_ref.shape[0]
    width = tiles_ref.shape[2]
    per_row = out_ref.shape[2] // width

    def issue(j, carry):
        block = order_ref[j]
        column = pl.multiple_of((block % per_row) * width, width)
        pltpu.make_async_copy(
            tiles_ref.at[j], out_ref.at[block // per_row, :, pl.ds(column, width)], sem
        ).start()
        return carry

    lax.fori_loop(0, count, issue, 0)
    pltpu.make_async_copy(out_ref, out_ref, sem).wait()


def dot(a, b, dims=((1,), (0,))):
    return lax.dot_general(a, b, (dims, ((), ())), preferred_element_type=jnp.float32)


def inverse_root(matrix):
    magnitude = jnp.sqrt(jnp.sum(matrix * matrix, keepdims=True)) + 1e-06
    m1 = matrix * (1.0 / magnitude)
    scale = lax.rsqrt(jnp.sqrt(magnitude))
    h1 = m1.astype(jnp.bfloat16)
    m2 = dot(h1, h1)
    m3 = dot(h1, m2.astype(jnp.bfloat16))
    high = COEFS[4] * m1 + COEFS[5] * m2 + COEFS[6] * m3
    top = dot(m3.astype(jnp.bfloat16), high.astype(jnp.bfloat16))
    size = matrix.shape[0]
    diagonal = lax.broadcasted_iota(jnp.int32, (size, size), 0) == lax.broadcasted_iota(
        jnp.int32, (size, size), 1
    )
    total = top + COEFS[1] * m1 + COEFS[2] * m2 + COEFS[3] * m3
    total = total + jnp.where(diagonal, COEFS[0], 0.0)
    return total * scale


def step_kernel(
    slots, dn, mn, block_count,
    order, grad_in, stats_in, roots_in,
    stats_out, roots_out, gathered_out,
    parts, recv, gathered, grads, stats, roots,
    rs_send, rs_recv, a1_send, a1_recv, a2_send, a2_recv, ag_send, ag_recv,
    in_sem, out_sem, part_sem, tile_sem,
):
    d = lax.axis_index("dp")
    m = lax.axis_index("mp")
    rows = grads.shape[1] // mn
    width = grads.shape[2]
    per_row = grad_in.shape[3] // width

    def pick(block, carry):
        column = pl.multiple_of((block % per_row) * width, width)
        pltpu.make_async_copy(
            grad_in.at[0, block // per_row, :, pl.ds(column, width)], parts.at[block], part_sem
        ).start()
        return carry

    lax.fori_loop(0, parts.shape[0], pick, 0)

    barrier = pltpu.get_barrier_semaphore()

    def greet(k, carry):
        pl.semaphore_signal(barrier, inc=1, device_id=(d, lax.rem(m + k, mn)), device_id_type=MESH)
        return carry

    lax.fori_loop(1, mn, greet, 0)

    @pl.when(d > 0)
    def _():
        pl.semaphore_signal(barrier, inc=1, device_id=(d - 1, m), device_id_type=MESH)

    @pl.when(d < dn - 1)
    def _():
        pl.semaphore_signal(barrier, inc=1, device_id=(d + 1, m), device_id_type=MESH)

    def stat_in(s, side):
        return pltpu.make_async_copy(stats_in.at[side, s], stats.at[side, s], in_sem.at[s, side])

    def root_in(s, side):
        return pltpu.make_async_copy(roots_in.at[side, s], roots.at[side, s], in_sem.at[s, 2 + side])

    def stat_out(s, side):
        return pltpu.make_async_copy(stats.at[side, s], stats_out.at[side, s], out_sem.at[s, side])

    def root_out(s, side):
        return pltpu.make_async_copy(roots.at[side, s], roots_out.at[side, s], out_sem.at[s, 2 + side])

    def fetch(s, carry):
        for side in range(2):
            root_in(s, side).start()
            stat_in(s, side).start()
        return carry

    lax.fori_loop(0, slots, fetch, 0)

    ends = (d == 0).astype(jnp.int32) + (d == dn - 1).astype(jnp.int32)
    pl.semaphore_wait(barrier, mn + 1 - ends)

    pltpu.make_async_copy(parts, parts, part_sem).wait()

    def rs_copy(s, o, step):
        place = o + 1 if step > 0 else o
        return pltpu.make_async_remote_copy(
            src_ref=recv.at[s, place],
            dst_ref=recv.at[s, place],
            send_sem=rs_send.at[s, place],
            recv_sem=rs_recv.at[s, place],
            device_id=(d + step, m),
            device_id_type=MESH,
        )

    def ag_copy(s, o, step):
        return pltpu.make_async_remote_copy(
            src_ref=gathered.at[s, o],
            dst_ref=gathered.at[s, o],
            send_sem=ag_send.at[s, o, 1 if step > 0 else 0],
            recv_sem=ag_recv.at[s, o],
            device_id=(d + step, m),
            device_id_type=MESH,
        )

    def rows_of(k):
        return pl.ds(pl.multiple_of(k * rows, rows), rows)

    def a1_copy(s, k):
        return pltpu.make_async_remote_copy(
            src_ref=recv.at[s, d, rows_of(k)],
            dst_ref=grads.at[s, rows_of(m)],
            send_sem=a1_send.at[s, k],
            recv_sem=a1_recv.at[s, m],
            device_id=(d, k),
            device_id_type=MESH,
        )

    def a2_copy(s, k):
        return pltpu.make_async_remote_copy(
            src_ref=recv.at[s, d + 1, rows_of(k)],
            dst_ref=gathered.at[s, d, rows_of(m)],
            send_sem=a2_send.at[s, k],
            recv_sem=a2_recv.at[s, m],
            device_id=(d, k),
            device_id_type=MESH,
        )

    def a1_arrival(s, k):
        return pltpu.make_async_copy(grads.at[s, rows_of(k)], grads.at[s, rows_of(k)], a1_recv.at[s, k])

    def a2_arrival(s, k):
        return pltpu.make_async_copy(
            gathered.at[s, d, rows_of(k)], gathered.at[s, d, rows_of(k)], a2_recv.at[s, k]
        )

    def peers(action):
        def body(k, carry):
            action(lax.rem(m + k, mn))
            return carry

        lax.fori_loop(1, mn, body, 0)

    def add_pieces(s, o, target, *terms):
        def body(p, carry):
            piece = parts[order[(s * dn + o) * mn + p]]
            at = rows_of(p)
            if terms:
                total = piece.astype(jnp.float32)
                for t in terms:
                    total = total + recv[s, t, at].astype(jnp.float32)
                piece = total.astype(jnp.bfloat16)
            recv[s, target, at] = piece
            return carry

        lax.fori_loop(0, mn, body, 0)

    def rs_start(s, rank):
        right, left = dn - 1 - rank, rank

        @pl.when((s < slots) & (d == 0))
        def _():
            add_pieces(s, right, right + 1)

            @pl.when(s > 0)
            def _():
                rs_copy(s - 1, right, 1).wait_send()

            rs_copy(s, right, 1).start()

        @pl.when((s < slots) & (d == dn - 1))
        def _():
            add_pieces(s, left, left)

            @pl.when(s > 0)
            def _():
                rs_copy(s - 1, left, -1).wait_send()

            rs_copy(s, left, -1).start()

    def relay_right(s, rank, turn):
        right = dn - 1 - rank

        @pl.when(turn & (s < slots) & (d > 0) & (d < right))
        def _():
            rs_copy(s, right, 1).wait_recv()
            add_pieces(s, right, right + 1, right + 1)
            rs_copy(s, right, 1).start()

    def relay_left(s, rank, turn):
        @pl.when(turn & (s < slots) & (d < dn - 1) & (d > rank))
        def _():
            rs_copy(s, rank, -1).wait_recv()
            add_pieces(s, rank, rank, rank)
            rs_copy(s, rank, -1).start()

    def forward(s, rank):
        near_left, near_right = d - 1 - rank, d + 1 + rank

        @pl.when((s >= 0) & (d < dn - 1) & (near_left >= 0))
        def _():
            ag_copy(s, near_left, 1).wait_recv()
            ag_copy(s, near_left, 1).start()

        @pl.when((s >= 0) & (d > 0) & (near_right < dn))
        def _():
            ag_copy(s, near_right, -1).wait_recv()
            ag_copy(s, near_right, -1).start()

    def own_sum(s):
        @pl.when(d > 0)
        def _():
            rs_copy(s, d, 1).wait_recv()

        @pl.when(d < dn - 1)
        def _():
            rs_copy(s, d, -1).wait_recv()

        @pl.when(d == 0)
        def _():
            add_pieces(s, d, d, d)

        @pl.when(d == dn - 1)
        def _():
            add_pieces(s, d, d, d + 1)

        @pl.when((d > 0) & (d < dn - 1))
        def _():
            add_pieces(s, d, d, d, d + 1)

        peers(lambda k: a1_copy(s, k).start())
        grads[s, rows_of(m)] = recv[s, d, rows_of(m)]

    def own_update(s):
        for side in range(2):
            root_in(s, side).wait()
        peers(lambda k: a1_arrival(s, k).wait())
        scaled = dot(roots[0, s], grads[s]).astype(jnp.bfloat16)
        recv[s, d + 1] = dot(scaled, roots[1, s]).astype(jnp.bfloat16)
        peers(lambda k: a2_copy(s, k).start())
        gathered[s, d, rows_of(m)] = recv[s, d + 1, rows_of(m)]

    def own_send(s):
        peers(lambda k: a2_arrival(s, k).wait())

        @pl.when(d < dn - 1)
        def _():
            ag_copy(s, d, 1).start()

        @pl.when(d > 0)
        def _():
            ag_copy(s, d, -1).start()

    def statistic(s, side):
        live = (s * dn + d) * mn + m < block_count
        stat_in(s, side).wait()
        block = grads[s]
        gram = dot(block, block, ((1 - side,), (1 - side,)))
        new = DECAY * stats[side, s] + (1.0 - DECAY) * gram
        stats[side, s] = jnp.where(live, new, 0.0)
        root = inverse_root(new)
        roots[side, s] = jnp.where(live, root, 0.0).astype(jnp.bfloat16)
        stat_out(s, side).start()
        root_out(s, side).start()

    for rank in range(dn - 1):
        rs_start(0, rank)

    low = 2 * d < dn

    def step(s, carry):
        for rank in range(dn - 1):
            rs_start(s + 1, rank)
            relay_right(s, rank, low)
            relay_left(s, rank, jnp.logical_not(low))
        forward(s - 1, 0)

        @pl.when(s > 0)
        def _():
            statistic(s - 1, 0)

        for rank in range(dn - 1):
            relay_left(s, rank, low)
            relay_right(s, rank, jnp.logical_not(low))

        @pl.when(s < slots)
        def _():
            own_sum(s)

        @pl.when(s > 0)
        def _():
            statistic(s - 1, 1)

        @pl.when(s < slots)
        def _():
            own_update(s)
            own_send(s)

        for rank in range(1, dn - 1):
            forward(s - 1, rank)
        return carry

    lax.fori_loop(0, slots + 1, step, 0)

    def tile_out(s):
        return pltpu.make_async_copy(gathered.at[s], gathered_out.at[s], tile_sem.at[s])

    def finish(s, carry):
        for o in range(dn):
            @pl.when((o < d) & (d == dn - 1))
            def _():
                ag_copy(s, o, 1).wait_recv()

            @pl.when((o > d) & (d == 0))
            def _():
                ag_copy(s, o, -1).wait_recv()

        tile_out(s).start()
        for side in range(2):
            stat_out(s, side).wait()
            root_out(s, side).wait()
        peers(lambda k: a1_copy(s, k).wait_send())
        peers(lambda k: a2_copy(s, k).wait_send())
        for o in range(dn):
            @pl.when((o > d) & ((d > 0) | (s == slots - 1)))
            def _():
                rs_copy(s, o, 1).wait_send()

            @pl.when((o < d) & ((d < dn - 1) | (s == slots - 1)))
            def _():
                rs_copy(s, o, -1).wait_send()

            @pl.when((o <= d) & (d < dn - 1))
            def _():
                ag_copy(s, o, 1).wait_send()

            @pl.when((o >= d) & (d > 0))
            def _():
                ag_copy(s, o, -1).wait_send()

        return carry

    lax.fori_loop(0, slots, finish, 0)

    def drain(s, carry):
        tile_out(s).wait()
        return carry

    lax.fori_loop(0, slots, drain, 0)


def shards(grad_parts, statistics, prior_roots, block_order):
    dn = lax.axis_size("dp")
    mn = lax.axis_size("mp")
    width = statistics.shape[-1]
    slots = statistics.shape[1]
    rows = grad_parts.shape[2]
    block_count = block_order.shape[0]
    positions = slots * dn * mn
    chosen = block_order
    if positions > block_count:
        chosen = jnp.pad(block_order, (0, positions - block_count))
    anywhere = pl.BlockSpec(memory_space=pl.ANY)
    indices = pl.BlockSpec(memory_space=pltpu.SMEM)
    tile_bytes = positions * rows * width * 2
    dma = pltpu.SemaphoreType.DMA
    block = (width, width)
    new_stats, new_roots, gathered = pl.pallas_call(
        functools.partial(step_kernel, slots, dn, mn, block_count),
        out_shape=(
            jax.ShapeDtypeStruct((2, slots) + block, jnp.float32),
            jax.ShapeDtypeStruct((2, slots) + block, jnp.bfloat16),
            jax.ShapeDtypeStruct((slots, dn) + block, jnp.bfloat16),
        ),
        in_specs=[indices, anywhere, anywhere, anywhere],
        out_specs=(anywhere, anywhere, anywhere),
        scratch_shapes=[
            pltpu.VMEM((block_count, rows, width), jnp.bfloat16),
            pltpu.VMEM((slots, dn + 1) + block, jnp.bfloat16),
            pltpu.VMEM((slots, dn) + block, jnp.bfloat16),
            pltpu.VMEM((slots,) + block, jnp.bfloat16),
            pltpu.VMEM((2, slots) + block, jnp.float32),
            pltpu.VMEM((2, slots) + block, jnp.bfloat16),
            dma((slots, dn + 1)),
            dma((slots, dn + 1)),
            dma((slots, mn)),
            dma((slots, mn)),
            dma((slots, mn)),
            dma((slots, mn)),
            dma((slots, dn, 2)),
            dma((slots, dn)),
            dma((slots, 4)),
            dma((slots, 4)),
            dma,
            dma((slots,)),
        ],
        compiler_params=pltpu.CompilerParams(
            collective_id=0, has_side_effects=True, vmem_limit_bytes=62 * 1024 * 1024
        ),
        cost_estimate=pl.CostEstimate(
            flops=slots * 20 * width**3, bytes_accessed=10 * tile_bytes, transcendentals=0
        ),
    )(
        chosen,
        grad_parts,
        statistics.reshape((2, slots) + block),
        prior_roots.reshape((2, slots) + block),
    )
    update = pl.pallas_call(
        scatter_kernel,
        out_shape=jax.ShapeDtypeStruct(grad_parts.shape[1:], jnp.bfloat16),
        in_specs=[indices, anywhere],
        out_specs=pl.BlockSpec(memory_space=pltpu.VMEM),
        scratch_shapes=[pltpu.SemaphoreType.DMA],
        compiler_params=pltpu.CompilerParams(vmem_limit_bytes=40 * 1024 * 1024),
        cost_estimate=pl.CostEstimate(flops=0, bytes_accessed=2 * tile_bytes, transcendentals=0),
    )(block_order, gathered.reshape(positions, rows, width))
    return (
        new_stats.reshape(statistics.shape),
        new_roots.reshape(prior_roots.shape),
        update,
    )


def solution(mesh):
    placed = (
        P("dp", None, "mp", None),
        P(None, None, "dp", "mp", None, None),
        P(None, None, "dp", "mp", None, None),
        P(),
    )
    return jax.shard_map(
        shards,
        mesh=mesh,
        in_specs=placed,
        out_specs=(
            P(None, None, "dp", "mp", None, None),
            P(None, None, "dp", "mp", None, None),
            P(None, "mp", None),
        ),
        check_vma=False,
    )
```
